128 devices in a mesh: row: 16 (over y, z), col: 8 (over x, core).
Axes of the slice: x: 4, y: 4, z: 4, core: 2. Of those that a mesh axis runs over, the one named last changes fastest.
Arguments:
- anchor_mesh: float32 [2, 4096, 2048], P(None, 'row', 'col'), may hold values from -6 to 6
- stiffness: float32 [4096, 2048], P('row', 'col'), may hold values from 0.25 to 4
- tissue: int32 [4, 4096, 2048], P(None, 'row', 'col'), may hold values 0 or 1
- flow_blocks: float32 [4, 16384, 2, 256], P(None, ('row', 'col')), may hold values from -8 to 8
- confidence: float32 [4, 16384, 256], P(None, ('row', 'col')), may hold values from 0.25 to 2
- flow_dest: int32 [4, 16384, 1], P(None, ('row', 'col')), may hold values from 0 to 127; in each aligned block of 128 rows (0 to 127, 128 to 255, ..., all dimensions but the last counted through in order) at most 2 rows name the same one
- flow_slot: int32 [4, 16384], P(None, ('row', 'col')), may hold values from 0 to 255
Outputs:
- relaxed: float32 [4, 2, 4096, 2048], P(None, None, 'row', 'col')
The draws below stay inside these ranges and needn't reach their ends.
Inputs may be any that keep to these rules, and one draw needn't show every extreme that they name: `flow_dest`: among the 128 blocks of one section held by one device, at most 2 name the same tile; in every draw some tile is named exactly 2 times so. Several blocks may land on the same square.
All inputs are finite; a program needn't handle non-finite values. No bound on the sum of `tissue` on one device may be relied on, other than what follows from the above.
Results may differ from the reference program's by a relative error of at most 0.0001.
Values sent between devices are 32-bit elements; how exact they have to be, the bound alone decides.
No kernel may reach another device: no remote copies, remote signals or barrier semaphores. Data moves between devices by JAX's collectives and lax.ppermute only.
A program may use at most 128 MiB of HBM per device.

```python
import math
from functools import reduce
import jax
import jax.numpy as jnp
import numpy as np

TILE_R = 256
TILE_C = 256
PB = 16
SECTIONS = 4
ITERS = 12
CAP = 2
BLK_DEV = 128
NR = 4096
NC = 2048
NBLK = 16384
POS = 256
N_ROW = 16
N_COL = 8


def touch_ends(array, rng, least, top_value):
    longest = array.shape.index(max(array.shape))
    spots = []
    for shift in (0, 1):
        where = [jax.random.randint(jax.random.fold_in(rng, axis), (), 0, length) for axis, length in enumerate(array.shape)]
        where[longest] = (where[longest] + shift) % array.shape[longest]
        spots.append(tuple(where))
    return array.at[spots[0]].set(least).at[spots[1]].set(top_value)


def level_of(rng, dims, split, least, top_value):
    loudness = 1.0
    for dim, parts in split:
        heights = jax.random.uniform(jax.random.fold_in(jax.random.fold_in(rng, 6), dim), (parts,), jnp.float32, least / len(split), top_value / len(split))
        loudness = loudness * jnp.repeat(jnp.exp(heights), dims[dim] // parts).reshape((-1,) + (1,) * (len(dims) - 1 - dim))
    return loudness


def deal_out(own_key, own, number, rows, number_of, top, limit, lean):
    order = jax.random.permutation(own_key, number_of)
    heavy_load, usual = portions_of(number_of, rows * top, limit, lean, True), portions_of(number_of, rows * top, limit, lean, False)
    places = jnp.arange(number_of)

    def named(sizes, rotation):
        used = int((sizes > 0).sum())
        fixed = max(1, used // 4)
        moved = fixed + (places - fixed + rotation * (used - fixed)) % max(1, number_of - fixed)
        return jnp.zeros((number_of,), jnp.int32).at[order[jnp.where(places < fixed, places, moved)]].set(jnp.asarray(sizes, jnp.int32))

    sizes = jnp.where(number % 4 == 0, named(heavy_load, number // 4), named(usual, number - number // 4 - 1))
    mixed = jax.random.permutation(jax.random.fold_in(own, 3), number_of)
    source_of, taker = mixed[0:number_of // 2 * 2:2], mixed[1:number_of // 2 * 2:2]
    room = jnp.minimum(sizes[source_of] - 1, limit - sizes[taker]) // 2
    room = jnp.where((source_of == order[0]) | (taker == order[0]) | (sizes[taker] == 0), 0, jnp.maximum(room, 0))
    moved = jax.random.randint(jax.random.fold_in(own, 4), (number_of // 2,), 0, 1 << 20) % (room + 1)
    sizes = sizes.at[source_of].add(-moved).at[taker].add(moved)
    members = jnp.searchsorted(jnp.cumsum(sizes), jnp.arange(rows * top), side="right").astype(jnp.int32)
    table = members.reshape(top, rows).T
    table = table[jax.random.permutation(jax.random.fold_in(own, 1), rows)]
    rotation = jax.random.randint(jax.random.fold_in(own, 2), (rows, 1), 0, top)
    return jnp.take_along_axis(table, (jnp.arange(top)[None, :] + rotation) % top, axis=1)


def portions_of(amount, total, limit, lean, full):
    weights = [(1 << 20) // math.isqrt(grade ** lean) + 1 for grade in range(1, amount + 1)]
    largest = limit if full else min(limit, max(-(-total // amount), total * weights[0] // sum(weights)))
    least = 1 if total - largest >= amount - 1 else 0
    counts, spare = [largest] + [least] * (amount - 1), total - largest - least * (amount - 1)
    while spare > 0:
        candidates = [i for i in range(1, amount) if counts[i] < largest] or [i for i in range(1, amount) if counts[i] < limit]
        mass, left = sum([weights[i] for i in candidates]), spare
        for i in candidates:
            addition = min(limit - counts[i], max(1, left * weights[i] // mass), spare)
            counts[i] = counts[i] + addition
            spare = spare - addition
    return np.array(counts)


def scatter_about(own_key, dims, scale, bound, split=(), held_as=jnp.bfloat16):
    gain = level_of(own_key, dims, split, -0.22, 0.18) if split else 1.0
    array = jax.random.normal(own_key, dims, jnp.float32) * scale * gain
    return jnp.minimum(jnp.maximum(array, -bound), bound).astype(held_as)


def setup_inputs(seed: int = 0) -> dict:
    keys = jax.random.split(jax.random.key(seed), 8)
    anchor_mesh = scatter_about(keys[0], (2, NR, NC), 1.0, 6.0, ((1, 16), (2, 8)), jnp.float32)
    stiffness = jnp.clip(jnp.exp(math.log(4.0) - 2.7725887 * jax.random.uniform(keys[1], (NR, NC), jnp.float32) ** level_of(keys[1], (NR, NC), ((0, 16), (1, 8)), -0.2, 0.2)), 0.25, 4.0)
    tissue = touch_ends((jax.random.randint(keys[2], (SECTIONS, NR, NC), 0, 4) < 3).astype(jnp.int32), jax.random.fold_in(keys[2], 1), 0, 1)
    flow_blocks = scatter_about(keys[3], (SECTIONS, NBLK, 2, PB * PB), 2.0, 8.0, ((1, 128),), jnp.float32)
    confidence = jnp.clip(jnp.exp(math.log(2.0) - 2.0794415 * jax.random.uniform(keys[4], (SECTIONS, NBLK, PB * PB), jnp.float32) ** level_of(keys[4], (SECTIONS, NBLK, PB * PB), ((1, 128),), -0.2, 0.2)), 0.25, 2.0)
    flow_dest_keys = jax.random.split(jax.random.fold_in(keys[5], 1), SECTIONS * NBLK // BLK_DEV)
    flow_dest_turns = jax.random.permutation(jax.random.fold_in(keys[5], 3), SECTIONS * NBLK // BLK_DEV)
    flow_dest = jax.vmap(lambda own, number: deal_out(jax.random.fold_in(keys[5], 2), own, number, BLK_DEV, N_ROW * N_COL, 1, CAP, 2))(flow_dest_keys, flow_dest_turns).reshape((SECTIONS, NBLK, 1))
    flow_slot = touch_ends(jax.random.randint(keys[6], (SECTIONS, NBLK), 0, POS), jax.random.fold_in(keys[6], 1), 0, POS - 1).astype(jnp.int32)
    return dict(anchor_mesh=anchor_mesh, stiffness=stiffness, tissue=tissue, flow_blocks=flow_blocks, confidence=confidence, flow_dest=flow_dest, flow_slot=flow_slot)


damping_weight = 0.8
anchor_weight = 0.5
neighbours = ((0, 1, 1.0), (0, -1, 1.0), (1, 0, 1.0), (-1, 0, 1.0), (1, 1, 0.5), (1, -1, 0.5), (-1, 1, 0.5), (-1, -1, 0.5))

def beside(padded, down, right):
    height = padded.shape[-2] - 2
    width = padded.shape[-1] - 2
    return padded[..., 1 + down:1 + down + height, 1 + right:1 + right + width]

def springs(padded_stiff):
    centre = beside(padded_stiff, 0, 0)
    return [jnp.sqrt(centre * beside(padded_stiff, down, right)) * share for down, right, share in neighbours]

def smoothing(padded):
    terms = [beside(padded, down, right) for down in (-1, 0, 1) for right in (-1, 0, 1)]
    return reduce(jnp.add, terms) / 9.0

def relax(padded, edges, diagonal, target):
    total = target
    for edge, (down, right, share) in zip(edges, neighbours):
        total = total + edge * beside(padded, down, right)
    centre = beside(padded, 0, 0)
    return centre + damping_weight * (total / diagonal - centre)

def reference(anchor_mesh, stiffness, tissue, flow_blocks, confidence, flow_dest, flow_slot):
    tiles = N_ROW * N_COL
    edges = springs(jnp.pad(stiffness, 1))
    total_edges = reduce(jnp.add, edges)
    border = ((0, 0), (1, 1), (1, 1))
    previous = anchor_mesh
    results = []
    for section in range(SECTIONS):
        place = (flow_dest[section, :, 0] * POS + flow_slot[section]).astype(jnp.int32)
        weights = confidence[section][:, None, :]
        payload = jnp.concatenate([flow_blocks[section] * weights, weights], axis=1)
        summed = jax.ops.segment_sum(payload, place, num_segments=tiles * POS)
        grid = summed.reshape(N_ROW, N_COL, TILE_R // PB, TILE_C // PB, 3, PB, PB)
        grid = grid.transpose(4, 0, 2, 5, 1, 3, 6).reshape(3, N_ROW * TILE_R, N_COL * TILE_C)
        mask = tissue[section].astype(jnp.float32)
        pulled = grid[:2] * mask
        weight = grid[2] * mask
        smooth = smoothing(jnp.pad(previous, border))
        diagonal = total_edges + weight + anchor_weight
        target = pulled + anchor_weight * smooth
        field = previous
        for sweep in range(ITERS):
            field = relax(jnp.pad(field, border), edges, diagonal, target)
        results.append(field)
        previous = field
    return jnp.stack(results)
```

```python
import jax
import jax.numpy as jnp
from jax import lax
from jax.experimental import pallas as pl
from jax.experimental.pallas import tpu as pltpu
from jax.sharding import PartitionSpec as P

SECTIONS = 4
ITERS = 12
TILES = 128
GROUP = (0, 1, 2, 3)
HALO = 48
WIDTHS = (48, 40, 24, 16)
LANES = (48, 36, 24, 12)
STEPS = 45
ROWS = 8 * STEPS
PITCH = 17
LINES = 49
ALL_WIDTHS = tuple(width for width in WIDTHS for _ in range(3)) + (HALO,) * 3
ALL_LANES = tuple(width for width in LANES for _ in range(3)) + (HALO,) * 3
DEPTH = 4

damping_weight = 0.8
anchor_weight = 0.5

f32 = jnp.float32
bf16 = jnp.bfloat16
VMEM_LIMIT = 24 * 1024 * 1024


def call(body, name, cost, out_shape, count, limit=VMEM_LIMIT, **more):
    if "in_specs" not in more:
        more["in_specs"] = whole(count)
    return pl.pallas_call(
        body,
        out_shape=out_shape,
        compiler_params=pltpu.CompilerParams(vmem_limit_bytes=limit),
        cost_estimate=pl.CostEstimate(flops=0, bytes_accessed=cost, transcendentals=0),
        name=name,
        **more,
    )


def whole(count):
    return [pl.BlockSpec(memory_space=pltpu.VMEM)] * count


def iota(shape, dim):
    return lax.broadcasted_iota(jnp.int32, shape, dim)


def ones_where(mask):
    return jnp.where(mask, 1.0, 0.0).astype(bf16)


def dot(a, b):
    return jnp.dot(a, b, preferred_element_type=f32)


def turned_dot(a, b):
    return lax.dot_general(a, b, (((1,), (1,)), ((), ())), preferred_element_type=f32)


def two_terms(a):
    high = a.astype(bf16)
    return jnp.concatenate([high, (a - high.astype(f32)).astype(bf16)], axis=0)


def earlier():
    return ones_where(iota((TILES, 128), 0) < iota((TILES, 128), 1))


def pack_kernel(group, flow_hbm, conf_hbm, dest_ref, slot_ref, out_ref, flow_ref, conf_ref, sems):
    copies = []
    for k, s in enumerate(group):
        copies.append(
            (
                pltpu.make_async_copy(conf_hbm.at[s], conf_ref.at[k], sems.at[2 * k]),
                pltpu.make_async_copy(flow_hbm.at[s], flow_ref.at[k], sems.at[2 * k + 1]),
            )
        )
        for copy in copies[-1]:
            copy.start()
    row_of = iota((TILES, 128), 0)
    before = earlier()
    places = jnp.zeros((TILES, 128), f32)
    for k, s in enumerate(group):
        named = row_of == dest_ref[s : s + 1, :]
        rank = dot(ones_where(named), before)
        ranked = [ones_where(named & (rank < 0.5)), ones_where(named & (rank > 0.5))]
        chosen = jnp.concatenate(ranked, axis=0)
        chosen = jnp.concatenate([chosen, chosen], axis=1)
        slot = slot_ref[s : s + 1, :].astype(f32)
        for r in range(2):
            places = places + turned_dot(ranked[r], jnp.where(row_of == 2 * k + r, slot, 0.0).astype(bf16))
        for copy in copies[k]:
            copy.wait()
        halves = [conf_ref[k, :, 128 * h : 128 * h + 128] for h in range(2)]
        for pair in range(3):
            if pair < 2:
                parts = [
                    halves[pair] * flow_ref[k, pl.ds(2 * pair + c, TILES, stride=4), :] for c in range(2)
                ]
            else:
                parts = halves
            sent = dot(chosen, two_terms(jnp.concatenate(parts, axis=1)))
            for r in range(2):
                for c in range(2):
                    out_ref[pl.ds(12 * k + 6 * r + 2 * pair + c, TILES, stride=LINES), :] = sent[
                        TILES * r : TILES * r + TILES, 128 * c : 128 * c + 128
                    ]
    out_ref[pl.ds(LINES - 1, TILES, stride=LINES), :] = places


def pack(group, flow, conf, dest, slot, limit=VMEM_LIMIT):
    count = len(group)
    return call(
        lambda *refs: pack_kernel(group, *refs),
        "pack",
        8 << 20,
        jax.ShapeDtypeStruct((TILES * LINES, 128), f32),
        4,
        limit=limit,
        in_specs=[pl.BlockSpec(memory_space=pltpu.HBM)] * 2 + whole(2),
        scratch_shapes=[
            pltpu.VMEM((count, 4 * TILES, 128), f32),
            pltpu.VMEM((count, TILES, 256), f32),
            pltpu.SemaphoreType.DMA((2 * count,)),
        ],
    )(flow, conf, dest, slot)


def exchanged_groups(v, lane):
    v = list(v)
    for bit in (4, 2, 1):
        right = (lane & (16 * bit)) != 0
        for a in range(8):
            if a & bit == 0:
                b = a | bit
                v[a], v[b] = (
                    jnp.where(right, pltpu.roll(v[b], 16 * bit, 1), v[a]),
                    jnp.where(right, v[b], pltpu.roll(v[a], 128 - 16 * bit, 1)),
                )
    return v


def land_kernel(group, arrived_ref, tissue_ref, *refs):
    *extras, out_ref, top_ref, bottom_ref, cells_ref = refs
    row = iota((256, TILES), 0)
    squares = ((row >> 7) * 128 + (row & 7) * 16 + ((row >> 3) & 15)).astype(f32)
    lane = iota((8, 128), 1)
    places = arrived_ref[pl.ds(LINES - 1, TILES, stride=LINES), :].astype(bf16)
    places = turned_dot(ones_where(iota((8, 128), 0) == iota((8, 128), 1)), places)
    offset = 0
    for k, s in enumerate(group):
        here = [ones_where(squares == places[2 * k + r : 2 * k + r + 1, :]) for r in range(2)]
        here = jnp.concatenate(here + here, axis=1)
        for pair in range(3):
            part = jnp.concatenate(
                [
                    jnp.concatenate(
                        [
                            arrived_ref[pl.ds(12 * k + 6 * r + 2 * pair + c, TILES, stride=LINES), :]
                            for c in range(2)
                        ],
                        axis=1,
                    )
                    for r in range(2)
                ],
                axis=0,
            )
            summed = dot(here, two_terms(part))
            for c in range(2):
                comp, half = (c, pair) if pair < 2 else (2, c)
                cells = summed[:, 128 * c : 128 * c + 128].reshape(2, 2, 8, 8, 128)
                for high in range(2):
                    for side in range(2):
                        turned = exchanged_groups([cells[high, side, i] for i in range(8)], lane)
                        for r in range(8):
                            rows = pl.ds(8 * PITCH * high + 8 * half + r, 8, stride=PITCH)
                            cells_ref[k, comp, side, rows, :] = turned[r]
        for side in range(2):
            for r in range(16):
                rows = slice(16 * r, 16 * r + 16)
                mask = tissue_ref[s, rows, 128 * side : 128 * side + 128].astype(f32)
                for comp in range(3):
                    value = cells_ref[k, comp, side, PITCH * r : PITCH * r + 16, :] * mask
                    out_ref[3 * k + comp, side, rows, :] = value
        width = WIDTHS[k]
        for comp in range(3):
            for side in range(2):
                cols = slice(128 * side, 128 * side + 128)
                top_ref[offset : offset + width, cols] = out_ref[3 * k + comp, side, :width, :]
                bottom_ref[offset : offset + width, cols] = out_ref[3 * k + comp, side, 256 - width :, :]
            offset += width
    for ref in extras:
        for i in range(ref.shape[0]):
            top_ref[offset : offset + HALO] = ref[i, :HALO]
            bottom_ref[offset : offset + HALO] = ref[i, 256 - HALO :]
            offset += HALO


def land(group, arrived, tissue, extras):
    count = len(group)
    strip = sum(ALL_WIDTHS)
    operands = [arrived, tissue, *extras]
    return call(
        lambda *refs: land_kernel(group, *refs),
        "land",
        16 << 20,
        [
            jax.ShapeDtypeStruct((count * 3, 2, 256, 128), f32),
            jax.ShapeDtypeStruct((strip, 256), f32),
            jax.ShapeDtypeStruct((strip, 256), f32),
        ],
        len(operands),
        scratch_shapes=[pltpu.VMEM((count, 3, 2, 16 * PITCH, 128), f32)],
    )(*operands)


def arranged(lanes):
    used, where = [], {}
    for width, i in sorted(((width, i) for i, width in enumerate(lanes)), key=lambda pair: -pair[0]):
        for half in range(2):
            block = next((n for n, taken in enumerate(used) if taken + width <= 128), len(used))
            if block == len(used):
                used.append(0)
            where[i, half] = (block, used[block])
            used[block] += width
    return where, len(used)


def plane_of(ref, i, rows, side):
    if len(ref.shape) == 4:
        return ref[i, side, rows, :]
    return ref[i, rows, 128 * side : 128 * side + 128]


def merge_strips(out_refs, height, strip_of):
    lane = iota((height, 128), 1)
    where, blocks = arranged(ALL_LANES)
    for side, out_ref in enumerate(out_refs):
        for block in range(blocks):
            merged = jnp.zeros((height, 128), f32)
            for (i, half), (at, offset) in where.items():
                if at != block:
                    continue
                strip = strip_of(i, half, side)
                turn = (offset + ALL_LANES[i] * side) % 128
                if turn:
                    strip = pltpu.roll(strip, turn, 1)
                merged = jnp.where((lane >= offset) & (lane < offset + ALL_LANES[i]), strip, merged)
            out_ref[block] = merged


def column_kernel(*refs):
    *own_refs, first_ref, last_ref = refs
    own = [(ref, i) for ref in own_refs for i in range(ref.shape[0])]

    def strip_of(i, half, side):
        ref, n = own[i]
        return plane_of(ref, n, slice(128 * half, 128 * half + 128), side)

    merge_strips((first_ref, last_ref), 128, strip_of)


def corner_kernel(above_ref, below_ref, first_ref, last_ref):
    starts = [sum(ALL_WIDTHS[:i]) for i in range(len(ALL_WIDTHS))]

    def strip_of(i, half, side):
        ref = below_ref if half else above_ref
        width = ALL_WIDTHS[i]
        strip = ref[starts[i] : starts[i] + width, 128 * side : 128 * side + 128]
        if width < HALO:
            strip = jnp.concatenate([strip, jnp.zeros((HALO - width, 128), f32)], axis=0)
        return strip

    merge_strips((first_ref, last_ref), HALO, strip_of)


def strips_of(kernel, name, height, operands):
    blocks = arranged(ALL_LANES)[1]
    return call(
        kernel,
        name,
        4 << 20,
        [jax.ShapeDtypeStruct((blocks, height, 128), f32)] * 2,
        len(operands),
        out_specs=whole(2),
    )(*operands)


def shifted(cells, axis, step):
    count = lax.axis_size(axis)
    pairs = [(i, i + step) for i in range(count) if 0 <= i + step < count]
    return lax.ppermute(cells, axis, pairs)


def ring(own, top, bottom):
    below = shifted(top, "row", -1)
    above = shifted(bottom, "row", 1)
    first, last = strips_of(column_kernel, "columns", 128, own)
    right = shifted(first, "col", -1)
    left = shifted(last, "col", 1)
    first, last = strips_of(corner_kernel, "corners", HALO, [above, below])
    right_corners = shifted(first, "col", -1)
    left_corners = shifted(last, "col", 1)
    return above, below, right, left, right_corners, left_corners


def fill(ext_ref, index, own, number, strips):
    above_ref, below_ref, *side_refs = strips
    own_ref, i = own
    width, start = ALL_WIDTHS[number], sum(ALL_WIDTHS[:number])
    where = arranged(ALL_LANES)[0]
    for plane in range(2):
        cols = slice(128 * plane, 128 * plane + 128)
        ext_ref[index, plane, HALO - width : HALO, :] = above_ref[start : start + width, cols]
        ext_ref[index, plane, HALO : HALO + 256, :] = plane_of(own_ref, i, slice(0, 256), plane)
        ext_ref[index, plane, HALO + 256 : HALO + 256 + width, :] = below_ref[start : start + width, cols]
    for half in range(2):
        at, offset = where[number, half]
        for refs, first, rows in (
            (side_refs[:2], HALO + 128 * half, 128),
            (side_refs[2:], HALO + 256 if half else HALO - width, width),
        ):
            right, left = refs[0][at, :rows, :], refs[1][at, :rows, :]
            if offset:
                right = pltpu.roll(right, 128 - offset, 1)
            if (offset + ALL_LANES[number]) % 128:
                left = pltpu.roll(left, 128 - offset - ALL_LANES[number], 1)
            near = iota((rows, 128), 1) < 64
            ext_ref[index, 2, first : first + rows, :] = jnp.where(near, right, left)


def spread(t):
    return pl.ds(t, 8, stride=STEPS)


def block(t):
    return slice(8 * t, 8 * t + 8)


def three(ref, index, t):
    if t < 0:
        return [pltpu.roll(v, 1, 0) for v in three(ref, index, STEPS - 1)]
    if t == STEPS:
        return [pltpu.roll(v, 7, 0) for v in three(ref, index, 0)]
    return [ref[index + (j, block(t))] for j in range(3)]


def walk(sources, body, late=1):
    here = [three(ref, index, 0) for ref, index in sources]
    above = [
        [p + q for p, q in zip(three(ref, index, -1), planes)]
        for (ref, index), planes in zip(sources, here)
    ]
    waiting = []
    for t in range(STEPS):
        ahead = [three(ref, index, t + 1) for ref, index in sources]
        below = [[p + q for p, q in zip(a, b)] for a, b in zip(here, ahead)]
        waiting.append(body(t, list(zip(here, above, below))))
        here, above = ahead, below
        if len(waiting) > late:
            for ref, at, value in waiting.pop(0):
                ref[at] = value
    for stores in waiting:
        for ref, at, value in stores:
            ref[at] = value


def relax_kernel(group, *refs):
    field_own, stiff_own, flow_own, *rest = refs
    strips, rest = rest[:6], rest[6:]
    out_ref, x_ref, g_ref, gi_ref, d_ref, f_ref, u0_ref, u1_ref, a_ref, c_ref, b_ref, stage_ref, sems = rest
    lane = iota((8, 128), 1)
    first_lane = lane == 0
    last_lane = lane == 127

    def from_left(planes):
        turned = [pltpu.roll(v, 1, 1) for v in planes]
        return [jnp.where(first_lane, turned[(j + 2) % 3], turned[j]) for j in range(3)]

    def from_right(planes):
        turned = [pltpu.roll(v, 127, 1) for v in planes]
        return [jnp.where(last_lane, turned[(j + 1) % 3], turned[j]) for j in range(3)]

    def weighted(above, below):
        v = [p + q for p, q in zip(above, below)]
        return [(p + q) + (w + w) for p, q, w in zip(from_left(v), from_right(v), v)]

    for c in range(2):
        fill(x_ref, c, (field_own, c), 3 * len(group) + c, strips)
    fill(x_ref, 2, (stiff_own, 0), 3 * len(group) + 2, strips)
    for t in range(STEPS):
        for j in range(3):
            stiff = x_ref[2, j, spread(t), :]
            root = jnp.sqrt(stiff)
            inside = stiff > 0
            g_ref[j, block(t), :] = root
            gi_ref[j, block(t), :] = jnp.where(inside, 1.0 / jnp.where(inside, root, 1.0), 0.0)
            for c in range(2):
                value = x_ref[c, j, spread(t), :]
                f_ref[c, j, block(t), :] = value
                u0_ref[c, j, block(t), :] = root * value

    def stiffness_sums(t, sources):
        ((here, above, below),) = sources
        z = weighted(above, below)
        return [
            (d_ref, (j, block(t)), here[j] * (0.5 * z[j] - 2.0 * here[j]) + anchor_weight)
            for j in range(3)
        ]

    walk([(g_ref, ())], stiffness_sums)

    copies = []
    for k, s in enumerate(group):
        for i in range(3):
            fill(x_ref, i, (flow_own, 3 * k + i), 3 * k + i, strips)

        def coefficients(t, sources):
            stores = []
            wg = []
            for j in range(3):
                root = g_ref[j, block(t), :]
                w = damping_weight / (d_ref[j, block(t), :] + x_ref[2, j, spread(t), :])
                wg.append(w * root)
                a = (0.5 * wg[j]) * root
                stores.append((a_ref, (j, block(t)), a))
                stores.append((c_ref, (j, block(t)), (1.0 - damping_weight) - 4.0 * a))
            for c, (here, above, below) in enumerate(sources):
                v = [(p + q) - h for p, q, h in zip(above, below, here)]
                sides = [p + q for p, q in zip(from_left(v), from_right(v))]
                for j in range(3):
                    target = x_ref[c, j, spread(t), :] + (anchor_weight / 9.0) * (sides[j] + v[j])
                    stores.append((b_ref, (c, j, block(t)), wg[j] * target))
            return stores

        walk([(f_ref, (c,)) for c in range(2)], coefficients)

        def sweep(src_ref, dst_ref):
            here = [three(src_ref, (c,), 0) for c in range(2)]
            above = [
                [p + q for p, q in zip(three(src_ref, (c,), -1), here[c])] for c in range(2)
            ]
            begun = []
            for t in range(STEPS + DEPTH):
                if t < STEPS:
                    ahead = [three(src_ref, (c,), t + 1) for c in range(2)]
                    below = [[p + q for p, q in zip(here[c], ahead[c])] for c in range(2)]
                    entry = []
                    a = [a_ref[j, block(t), :] for j in range(3)]
                    keep = [c_ref[j, block(t), :] for j in range(3)]
                    twice = [w + w for w in a]
                    for c in range(2):
                        v = [p + q for p, q in zip(above[c], below[c])]
                        right = [pltpu.roll(w, 1, 1) for w in v]
                        left = [pltpu.roll(w, 127, 1) for w in v]
                        known = [
                            (keep[j] * here[c][j] + b_ref[c, j, block(t), :]) + twice[j] * v[j]
                            for j in range(3)
                        ]
                        entry.append((known, right, left))
                    begun.append(entry)
                    here, above = ahead, below
                if t >= DEPTH:
                    at = t - DEPTH
                    a = [a_ref[j, block(at), :] for j in range(3)]
                    for c, (known, right, left) in enumerate(begun.pop(0)):
                        for j in range(3):
                            sides = jnp.where(first_lane, right[(j + 2) % 3], right[j]) + jnp.where(
                                last_lane, left[(j + 1) % 3], left[j]
                            )
                            dst_ref[c, j, block(at), :] = known[j] + a[j] * sides

        def two(i, carry):
            sweep(u0_ref, u1_ref)
            sweep(u1_ref, u0_ref)
            return carry

        lax.fori_loop(0, ITERS // 2, two, 0)

        for t in range(STEPS):
            for j in range(3):
                inverse = gi_ref[j, block(t), :]
                for c in range(2):
                    value = inverse * u0_ref[c, j, block(t), :]
                    f_ref[c, j, block(t), :] = value
                    x_ref[c, j, spread(t), :] = value
        for c in range(2):
            for j in range(2):
                cols = slice(128 * j, 128 * j + 128)
                value = x_ref[c, j, HALO : HALO + 256, :]
                stage_ref[k, c, :, cols] = value
        copy = pltpu.make_async_copy(stage_ref.at[k], out_ref.at[s], sems.at[k])
        copy.start()
        copies.append(copy)
    for copy in copies:
        copy.wait()


def relax(group, field, stiffness, flow, strips):
    ext = (3, ROWS, 128)
    operands = [field, stiffness, flow, *strips]
    return call(
        lambda *refs: relax_kernel(group, *refs),
        "relax",
        96 << 20,
        jax.ShapeDtypeStruct((SECTIONS, 2, 256, 256), f32),
        len(operands),
        out_specs=pl.BlockSpec(memory_space=pl.ANY),
        scratch_shapes=[
            pltpu.VMEM((3,) + ext, f32),
            pltpu.VMEM(ext, f32),
            pltpu.VMEM(ext, f32),
            pltpu.VMEM(ext, f32),
            pltpu.VMEM((2,) + ext, f32),
            pltpu.VMEM((2,) + ext, f32),
            pltpu.VMEM((2,) + ext, f32),
            pltpu.VMEM(ext, f32),
            pltpu.VMEM(ext, f32),
            pltpu.VMEM((2,) + ext, f32),
            pltpu.VMEM((len(group), 2, 256, 256), f32),
            pltpu.SemaphoreType.DMA((len(group),)),
        ],
    )(*operands)


def shards(anchor_mesh, stiffness, tissue, flow_blocks, confidence, flow_dest, flow_slot):
    flow = (
        flow_blocks.reshape(SECTIONS, TILES, 2, 2, 128).transpose(0, 1, 3, 2, 4).reshape(SECTIONS, 4 * TILES, 128)
    )
    dest = flow_dest.reshape(SECTIONS, TILES)

    def exchanged(buffer):
        buffer = buffer.reshape(TILES, LINES, 1, 128)
        arrived = lax.all_to_all(buffer, ("row", "col"), split_axis=0, concat_axis=0, tiled=True)
        return arrived.reshape(TILES * LINES, 128)

    stiffness = stiffness[None]
    arrived = exchanged(pack(GROUP, flow, confidence, dest, flow_slot, 56 << 20))
    pulled, top, bottom = land(GROUP, arrived, tissue, [anchor_mesh, stiffness])
    strips = ring([pulled, anchor_mesh, stiffness], top, bottom)
    return relax(GROUP, anchor_mesh, stiffness, pulled, strips)


def solution(mesh):
    placed = (
        P(None, "row", "col"),
        P("row", "col"),
        P(None, "row", "col"),
        P(None, ("row", "col"), None, None),
        P(None, ("row", "col"), None),
        P(None, ("row", "col"), None),
        P(None, ("row", "col")),
    )
    return jax.shard_map(
        shards, mesh=mesh, in_specs=placed, out_specs=P(None, None, "row", "col"), check_vma=False
    )
```
